512 devices in a mesh: mem: 32 (over z, x), geo: 16 (over y, core).
Axes of the slice: x: 4, y: 8, z: 8, core: 2. Of those that a mesh axis runs over, the one named last changes fastest.
Arguments:
- control: float32 [32, 32, 48, 384], P('mem', 'geo'), may hold values from -6 to 6
- kappa_table: float32 [16], replicated, may hold values from 0.02 to 0.24
- kappa_index: int32 [48, 384], replicated, may hold values from 0 to 15
- tile_bounds: int32 [17], replicated, may hold values from 0 to 18432, as said below
- filter_bands: float32 [16, 5, 32], replicated, may hold values from -0.3 to 0.3
- perturbation: bfloat16 [2, 32, 32, 18432], P(None, 'mem', None, 'geo'), may hold values from -6 to 6
Outputs:
- increment: float32 [2, 32, 18432], P(None, 'mem', 'geo')
The draws below stay inside these ranges and needn't reach their ends.
Inputs may be any that keep to these rules, and one draw needn't show every extreme that they name: tile_bounds[0] is 0, tile_bounds[16] is 18432, and the bounds never fall; tile t holds columns tile_bounds[t] to tile_bounds[t + 1] - 1.
All inputs are finite; a program needn't handle non-finite values.
Results may differ from the reference program's by a relative error of at most 0.005.
Values may be sent and summed in bfloat16 or wider, within the bound.
No kernel may reach another device: no remote copies, remote signals or barrier semaphores. Data moves between devices by JAX's collectives and lax.ppermute only.
A program may use at most 64 MiB of HBM per device.

```python
import math
import jax
import jax.numpy as jnp
from jax import lax

LEV = 32
HX = 48
HY = 384
ITERS = 10
KAPPAS = 16
MEMBERS = 32
TILES = 16
NCOL = 18432


def draw_tile_bounds(key, part):
    widths = jax.random.randint(jax.random.fold_in(key, 7), (TILES,), 1, 5)
    cumulative = jnp.cumsum(widths).astype(jnp.int32)
    interior = HX * HY * cumulative // cumulative[-1]
    return jnp.concatenate([jnp.zeros((1,), jnp.int32), interior.astype(jnp.int32)])


def plant(array, key, least, largest):
    longest = array.shape.index(max(array.shape))
    spots = []
    for shift in (0, 1):
        where = [jax.random.randint(jax.random.fold_in(key, axis), (), 0, length) for axis, length in enumerate(array.shape)]
        where[longest] = (where[longest] + shift) % array.shape[longest]
        spots.append(tuple(where))
    return array.at[spots[0]].set(least).at[spots[1]].set(largest)


def raised(array, rng, source, target, parts, factor):
    owner, partner = [(jnp.arange(array.shape[position]) // (array.shape[position] // parts)).reshape([-1 if axis == position else 1 for axis in range(array.ndim)]) for position in (source, target)]
    chosen = jax.random.permutation(rng, parts)[partner]
    strong = (owner == chosen) | (owner == (partner + parts // 2) % parts)
    return jnp.where(strong, factor * array, array)


def shard_levels(own_key, dims, shards, least, high):
    gain = 1.0
    for axis_at, blocks in shards:
        steps = jax.random.uniform(jax.random.fold_in(jax.random.fold_in(own_key, 6), axis_at), (blocks,), jnp.float32, least / len(shards), high / len(shards))
        gain = gain * jnp.repeat(jnp.exp(steps), dims[axis_at] // blocks).reshape((-1,) + (1,) * (len(dims) - 1 - axis_at))
    return gain


def normal_values(stream_key, dims, spread, reach, cuts=(), kind=jnp.bfloat16):
    level = shard_levels(stream_key, dims, cuts, -0.22, 0.18) if cuts else 1.0
    entries = jax.random.normal(stream_key, dims, jnp.float32) * spread * level
    return jnp.minimum(jnp.maximum(entries, -reach), reach).astype(kind)


def heavy_noise(stream_key, extent, width, limit, pieces, heavy, kind=jnp.bfloat16):
    values = width * jax.random.normal(stream_key, extent, jnp.float32)
    if pieces:
        values = values * shard_levels(stream_key, extent, pieces, -0.22, 0.18)
    return jnp.clip(raised(values, jax.random.fold_in(stream_key, 3), *heavy), -limit, limit).astype(kind)


def setup_inputs(seed: int = 0) -> dict:
    keys = jax.random.split(jax.random.key(seed), 7)
    control = normal_values(keys[0], (MEMBERS, LEV, HX, HY), 1.0, 6.0, ((0, 32), (1, 16)), jnp.float32)
    kappa_table = jnp.clip(jnp.exp(jax.random.uniform(keys[1], (KAPPAS,), jnp.float32, math.log(0.02), math.log(0.24))), 0.02, 0.24)
    kappa_index = plant(jax.random.randint(keys[2], (HX, HY), 0, KAPPAS), jax.random.fold_in(keys[2], 1), 0, KAPPAS - 1).astype(jnp.int32)
    tile_bounds = draw_tile_bounds(jax.random.fold_in(keys[6], 71), 0)
    filter_bands = jnp.clip(jax.random.uniform(keys[4], (TILES, 5, LEV), jnp.float32, -0.3, 0.3), -0.3, 0.3)
    perturbation = heavy_noise(keys[5], (2, MEMBERS, LEV, NCOL), 1.0, 6.0, ((1, 32), (3, 16)), (1, 2, 32, 2.75))
    return {"control": control, "kappa_table": kappa_table, "kappa_index": kappa_index, "tile_bounds": tile_bounds, "filter_bands": filter_bands, "perturbation": perturbation}


def neighbours(state):
    east = jnp.concatenate([state[..., 1:, :], state[..., -1:, :]], axis=-2)
    west = jnp.concatenate([state[..., :1, :], state[..., :-1, :]], axis=-2)
    north = jnp.concatenate([state[..., 1:], state[..., -1:]], axis=-1)
    south = jnp.concatenate([state[..., :1], state[..., :-1]], axis=-1)
    return east, west, north, south


def face_weights(kappa_field):
    return tuple(0.5 * (kappa_field + other) for other in neighbours(kappa_field))


def diffuse_step(state, weights):
    east, west, north, south = neighbours(state)
    update = weights[0] * (east - state) + weights[1] * (west - state)
    update = update + weights[2] * (north - state) + weights[3] * (south - state)
    return state + update


def vertical_filter(values, coefficients):
    levels = values.shape[0]
    padded = jnp.pad(values, ((2, 2), (0, 0)))
    result = values
    for offset in range(5):
        result = result + coefficients[offset] * padded[offset:offset + levels]
    return result


def reference(control, kappa_table, kappa_index, tile_bounds, filter_bands, perturbation):
    kappa_field = kappa_table[kappa_index]
    weights = face_weights(kappa_field)
    columns = jnp.arange(HX * HY, dtype=jnp.int32)
    tile_ids = jnp.sum((columns[None, :] >= tile_bounds[1:-1][:, None]).astype(jnp.int32), axis=0).astype(jnp.int32)
    coefficients = jnp.transpose(filter_bands[tile_ids], (1, 2, 0))

    def one_member(member_field):
        state_field = lax.fori_loop(0, ITERS, lambda step, cur: diffuse_step(cur, weights), member_field)
        flattened = state_field.reshape(LEV, HX * HY)
        return vertical_filter(flattened, coefficients).astype(jnp.bfloat16)

    filtered = lax.map(one_member, control)

    def accumulate(running, members_pair):
        member_filtered, member_pert = members_pair
        return running + member_pert.astype(jnp.float32) * member_filtered.astype(jnp.float32)[None], None

    running, unused = lax.scan(accumulate, jnp.zeros((2, LEV, HX * HY), jnp.float32), (filtered, jnp.moveaxis(perturbation, 1, 0)))
    return running
```

```python
import jax
import jax.numpy as jnp
from jax import lax
from jax.experimental import pallas as pl
from jax.experimental.pallas import tpu as pltpu
from jax.sharding import PartitionSpec as P

ITERS = 10
LANES = 128
VMEM = pl.BlockSpec(memory_space=pltpu.VMEM)
SMEM = pl.BlockSpec(memory_space=pltpu.SMEM)


def diffuse_kernel(control_ref, table_ref, index_ref, out_ref, rows_ref):
    levels, height, width = control_ref.shape[1:]
    groups = out_ref.shape[0]
    phases = height // groups
    lane_tiles = width // LANES

    def phase(load, r):
        for k in range(lane_tiles):
            rows_ref[k] = load(k)
        return [rows_ref[k, pl.ds(r, groups, stride=phases), :] for k in range(lane_tiles)]

    def split(load):
        for k in range(lane_tiles):
            rows_ref[k] = load(k)
        return [
            jnp.concatenate(
                [rows_ref[k, pl.ds(r, groups, stride=phases), :] for k in range(lane_tiles)], axis=1
            )
            for r in range(phases)
        ]

    def kappa_tile(k):
        index = index_ref[:, k * LANES : (k + 1) * LANES]
        value = jnp.zeros(index.shape, jnp.float32)
        for entry in range(table_ref.shape[0]):
            value = jnp.where(index == entry, table_ref[entry], value)
        return value

    def right(x):
        return pltpu.roll(x, width - 1, 1)

    def left(x):
        return pltpu.roll(x, 1, 1)

    def down(x):
        return pltpu.roll(x, groups - 1, 0)

    def up(x):
        return pltpu.roll(x, 1, 0)

    kappa = split(kappa_tile)
    column = lax.broadcasted_iota(jnp.int32, (groups, width), 1)
    group = lax.broadcasted_iota(jnp.int32, (groups, width), 0)
    north = [jnp.where(column < width - 1, 0.5 * (k + right(k)), 0.0) for k in kappa]
    east = [0.5 * (kappa[r] + kappa[r + 1]) for r in range(phases - 1)]
    last = 0.5 * (kappa[phases - 1] + down(kappa[0]))
    east.append(jnp.where(group < groups - 1, last, 0.0))

    for level in range(levels):
        state = split(lambda k: control_ref[0, level, :, k * LANES : (k + 1) * LANES])
        for step in range(ITERS):
            flux_n = [north[r] * (right(state[r]) - state[r]) for r in range(phases)]
            after = state[1:] + [down(state[0])]
            flux_e = [east[r] * (after[r] - state[r]) for r in range(phases)]
            before = [up(flux_e[phases - 1])] + flux_e[:-1]
            state = [
                state[r] + (flux_e[r] - before[r]) + (flux_n[r] - left(flux_n[r]))
                for r in range(phases)
            ]
        for r in range(phases):
            value = state[r].astype(jnp.bfloat16)
            out_ref[:, level, r * width : (r + 1) * width] = value


def diffuse(control, table, index, groups):
    levels, height, width = control.shape[1:]
    return pl.pallas_call(
        diffuse_kernel,
        out_shape=jax.ShapeDtypeStruct((groups, levels, height * width // groups), jnp.bfloat16),
        in_specs=[VMEM, SMEM, VMEM],
        out_specs=VMEM,
        scratch_shapes=[pltpu.VMEM((width // LANES, height, LANES), jnp.float32)],
        name="diffuse",
    )(control, table, index)


def product_kernel(state_ref, coef_ref, pert_ref, out_ref, pad_ref):
    shards, share, width = state_ref.shape
    levels = shards * share
    tiles = width // LANES
    bands = coef_ref.shape[0]
    margin = 8
    for c in range(tiles):
        lanes = slice(c * LANES, (c + 1) * LANES)
        pad_ref[c, 0:margin] = jnp.zeros((margin, LANES), jnp.float32)
        pad_ref[c, margin + levels : 2 * margin + levels] = jnp.zeros((margin, LANES), jnp.float32)
        for g in range(shards):
            pad_ref[c, margin + g * share : margin + (g + 1) * share] = state_ref[g, :, lanes].astype(jnp.float32)
        value = pad_ref[c, margin : margin + levels]
        for k in range(bands):
            start = margin + k - bands // 2
            value = value + coef_ref[k, :, lanes] * pad_ref[c, start : start + levels]
        for v in range(2):
            product = pert_ref[v, 0, :, lanes].astype(jnp.float32) * value
            out_ref[:, v, lanes] = product.astype(jnp.bfloat16)


def products(state, coefficients, perturbation):
    shards, share, width = state.shape
    levels = shards * share
    return pl.pallas_call(
        product_kernel,
        out_shape=jax.ShapeDtypeStruct((levels, 2, width), jnp.bfloat16),
        in_specs=[VMEM, VMEM, VMEM],
        out_specs=VMEM,
        scratch_shapes=[pltpu.VMEM((width // LANES, levels + 16, LANES), jnp.float32)],
        name="products",
    )(state, coefficients, perturbation)


def sum_kernel(terms_ref, out_ref):
    total = terms_ref[0].astype(jnp.float32)
    for m in range(1, terms_ref.shape[0]):
        total = total + terms_ref[m].astype(jnp.float32)
    for v in range(2):
        out_ref[v] = total[v : v + 1]


def total(terms):
    return pl.pallas_call(
        sum_kernel,
        out_shape=jax.ShapeDtypeStruct((terms.shape[1], 1, terms.shape[2]), jnp.float32),
        in_specs=[VMEM],
        out_specs=VMEM,
        name="total",
    )(terms)


def coefficients_of(tile_bounds, filter_bands, width):
    tiles = filter_bands.shape[0]
    columns = lax.axis_index("geo") * width + jnp.arange(width, dtype=jnp.int32)
    tile_ids = jnp.sum((columns[None, :] >= tile_bounds[1:-1][:, None]).astype(jnp.int32), axis=0)
    one_hot = (tile_ids[None, :] == jnp.arange(tiles, dtype=jnp.int32)[:, None]).astype(jnp.float32)
    return jnp.einsum("tkl,tc->klc", filter_bands, one_hot, precision=lax.Precision.HIGHEST)


def solution(mesh):
    groups = mesh.shape["geo"]

    def body(control, kappa_table, kappa_index, tile_bounds, filter_bands, perturbation):
        sent = diffuse(control, kappa_table, kappa_index, groups)
        state = lax.all_to_all(sent, "geo", 0, 0, tiled=True)
        coefficients = coefficients_of(tile_bounds, filter_bands, state.shape[2])
        terms = products(state, coefficients, perturbation)
        return total(lax.all_to_all(terms, "mem", 0, 0, tiled=True))

    in_specs = (P("mem", "geo", None, None), P(), P(), P(), P(), P(None, "mem", None, "geo"))
    out_specs = P(None, "mem", "geo")
    return jax.shard_map(body, mesh=mesh, in_specs=in_specs, out_specs=out_specs, check_vma=False)
```

```python
import jax
import jax.numpy as jnp
from jax import lax
from jax.experimental import pallas as pl
from jax.experimental.pallas import tpu as pltpu
from jax.sharding import PartitionSpec as P

ITERS = 10
LANES = 128
HBM = pl.BlockSpec(memory_space=pltpu.HBM)
VMEM = pl.BlockSpec(memory_space=pltpu.VMEM)
SMALL = pltpu.CompilerParams(vmem_limit_bytes=4 << 20)


def coefficients(bounds_ref, bands_ref, out_ref):
    tiles = bands_ref.shape[1]
    width = out_ref.shape[2]
    first = lax.axis_index("geo") * width
    column = first + lax.broadcasted_iota(jnp.int32, (tiles, width), 1)
    tile = jnp.zeros((tiles, width), jnp.int32)
    for j in range(1, tiles):
        tile = tile + (column >= bounds_ref[j]).astype(jnp.int32)
    own = (tile == lax.broadcasted_iota(jnp.int32, (tiles, width), 0)).astype(jnp.float32)
    own = own.astype(jnp.bfloat16)
    for k in range(out_ref.shape[0]):
        rest = bands_ref[k]
        value = 0.0
        for part in range(3):
            piece = rest.astype(jnp.bfloat16)
            rest = rest - piece.astype(jnp.float32)
            value = value + lax.dot_general(
                piece, own, (((0,), (0,)), ((), ())), preferred_element_type=jnp.float32
            )
        out_ref[k] = value


def diffuse_kernel(
    control_hbm,
    table_hbm,
    index_hbm,
    bounds_hbm,
    bands_hbm,
    out_ref,
    coef_ref,
    control_ref,
    table_ref,
    index_ref,
    bounds_ref,
    bands_ref,
    rows_ref,
    sems,
):
    copies = [
        pltpu.make_async_copy(source, target, sems.at[i])
        for i, (source, target) in enumerate(
            (
                (bounds_hbm, bounds_ref),
                (bands_hbm, bands_ref),
                (table_hbm, table_ref),
                (index_hbm, index_ref),
                (control_hbm, control_ref),
            )
        )
    ]
    for copy in copies:
        copy.start()
    levels, height, width = control_ref.shape[1:]
    groups = out_ref.shape[0]
    phases = height // groups
    tiles = width // LANES
    each = range(phases)

    def split(slot, load):
        for k in range(tiles):
            rows_ref[slot, k] = load(slice(k * LANES, (k + 1) * LANES))
        return [
            jnp.concatenate(
                [rows_ref[slot, k, pl.ds(r, groups, stride=phases), :] for k in range(tiles)],
                axis=1,
            )
            for r in each
        ]

    def kappa_of(lanes):
        index = index_ref[:, lanes]
        values = [table_ref[entry] for entry in range(table_ref.shape[0])]
        bit = 1
        while len(values) > 1:
            odd = (index & bit) != 0
            values = [jnp.where(odd, b, a) for a, b in zip(values[::2], values[1::2])]
            bit *= 2
        return values[0]

    def north_of(x):
        return pltpu.roll(x, width - 1, 1)

    def south_of(x):
        return pltpu.roll(x, 1, 1)

    def next_group(x):
        return pltpu.roll(x, groups - 1, 0)

    def previous_group(x):
        return pltpu.roll(x, 1, 0)

    copies[0].wait()
    copies[1].wait()
    coefficients(bounds_ref, bands_ref, coef_ref)
    copies[2].wait()
    copies[3].wait()
    kappa = split(levels, kappa_of)
    column = lax.broadcasted_iota(jnp.int32, (groups, width), 1)
    group = lax.broadcasted_iota(jnp.int32, (groups, width), 0)
    north = [jnp.where(column < width - 1, 0.5 * (k + north_of(k)), 0.0) for k in kappa]
    south = [south_of(w) for w in north]
    east = [0.5 * (kappa[r] + kappa[r + 1]) for r in range(phases - 1)]
    last = 0.5 * (kappa[-1] + next_group(kappa[0]))
    east.append(jnp.where(group < groups - 1, last, 0.0))
    west = [previous_group(east[-1])] + east[:-1]
    own = [1.0 - ((east[r] + west[r]) + (north[r] + south[r])) for r in each]

    def step(state):
        after = state[1:] + [next_group(state[0])]
        before = [previous_group(state[-1])] + state[:-1]
        return [
            (own[r] * state[r] + (east[r] * after[r] + west[r] * before[r]))
            + (north[r] * north_of(state[r]) + south[r] * south_of(state[r]))
            for r in each
        ]

    copies[4].wait()
    states = [split(v, lambda lanes: control_ref[0, v, :, lanes]) for v in range(levels)]
    for _ in range(ITERS):
        states = [step(state) for state in states]
    for level in range(levels):
        for r in each:
            value = states[level][r].astype(jnp.bfloat16)
            out_ref[:, level, r * width : (r + 1) * width] = value


def diffuse(control, table, index, bounds, bands, groups):
    levels, height, width = control.shape[1:]
    share = height * width // groups
    arguments = [
        pltpu.with_memory_space_constraint(x, pltpu.HBM)
        for x in (control, table, index, bounds, bands)
    ]
    return pl.pallas_call(
        diffuse_kernel,
        out_shape=(
            jax.ShapeDtypeStruct((groups, levels, share), jnp.bfloat16),
            jax.ShapeDtypeStruct((bands.shape[0], bands.shape[2], share), jnp.float32),
        ),
        in_specs=[HBM] * 5,
        out_specs=(VMEM, VMEM),
        scratch_shapes=[
            pltpu.VMEM(control.shape, jnp.float32),
            pltpu.SMEM(table.shape, jnp.float32),
            pltpu.VMEM(index.shape, jnp.int32),
            pltpu.SMEM(bounds.shape, jnp.int32),
            pltpu.VMEM(bands.shape, jnp.float32),
            pltpu.VMEM((levels + 1, width // LANES, height, LANES), jnp.float32),
            pltpu.SemaphoreType.DMA((5,)),
        ],
        compiler_params=SMALL,
        name="diffuse",
    )(*arguments)


def product_kernel(state_ref, coef_ref, pert_ref, out_ref, pad_ref):
    shards, share, width = state_ref.shape
    levels = shards * share
    bands = coef_ref.shape[0]
    margin = 8
    for c in range(width // LANES):
        lanes = slice(c * LANES, (c + 1) * LANES)
        pad_ref[c, 0:margin] = jnp.zeros((margin, LANES), jnp.float32)
        pad_ref[c, margin + levels : 2 * margin + levels] = jnp.zeros((margin, LANES), jnp.float32)
        for g in range(shards):
            rows = slice(margin + g * share, margin + (g + 1) * share)
            pad_ref[c, rows] = state_ref[g, :, lanes].astype(jnp.float32)
        value = pad_ref[c, margin : margin + levels]
        for k in range(bands):
            start = margin + k - bands // 2
            value = value + coef_ref[k, :, lanes] * pad_ref[c, start : start + levels]
        for v in range(2):
            product = pert_ref[v, 0, :, lanes].astype(jnp.float32) * value
            out_ref[:, v, lanes] = product.astype(jnp.bfloat16)


def products(state, coefs, perturbation):
    shards, share, width = state.shape
    levels = shards * share
    return pl.pallas_call(
        product_kernel,
        out_shape=jax.ShapeDtypeStruct((levels, 2, width), jnp.bfloat16),
        in_specs=[VMEM, VMEM, VMEM],
        out_specs=VMEM,
        scratch_shapes=[pltpu.VMEM((width // LANES, levels + 16, LANES), jnp.float32)],
        compiler_params=SMALL,
        name="products",
    )(state, coefs, perturbation)


def sum_kernel(terms_ref, out_ref):
    total = terms_ref[0].astype(jnp.float32)
    for m in range(1, terms_ref.shape[0]):
        total = total + terms_ref[m].astype(jnp.float32)
    for v in range(2):
        out_ref[v] = total[v : v + 1]


def member_sum(terms):
    return pl.pallas_call(
        sum_kernel,
        out_shape=jax.ShapeDtypeStruct((terms.shape[1], 1, terms.shape[2]), jnp.float32),
        in_specs=[VMEM],
        out_specs=VMEM,
        compiler_params=SMALL,
        name="member_sum",
    )(terms)


def solution(mesh):
    groups = mesh.shape["geo"]

    def body(control, kappa_table, kappa_index, tile_bounds, filter_bands, perturbation):
        bands = jnp.transpose(filter_bands, (1, 0, 2))
        sent, coefs = diffuse(control, kappa_table, kappa_index, tile_bounds, bands, groups)
        state = lax.all_to_all(sent, "geo", 0, 0, tiled=True)
        terms = products(state, coefs, perturbation)
        return member_sum(lax.all_to_all(terms, "mem", 0, 0, tiled=True))

    in_specs = (P("mem", "geo", None, None), P(), P(), P(), P(), P(None, "mem", None, "geo"))
    out_specs = P(None, "mem", "geo")
    return jax.shard_map(body, mesh=mesh, in_specs=in_specs, out_specs=out_specs, check_vma=False)
```

```python
import functools

import jax
import jax.numpy as jnp
from jax import lax
from jax.experimental import pallas as pl
from jax.experimental.pallas import tpu as pltpu
from jax.sharding import PartitionSpec as P

ITERS = 10
LANES = 128
GEO_FIRST = 8
MEM_FIRST = 18
HBM = pl.BlockSpec(memory_space=pltpu.HBM)
VMEM = pl.BlockSpec(memory_space=pltpu.VMEM)
SMALL = pltpu.CompilerParams(vmem_limit_bytes=4 << 20)


def group_order(size, first):
    return [(first + place) % size for place in range(size)]


def store_turned(out_ref, value, first, *where):
    rows = value.shape[0]
    value = value.astype(out_ref.dtype)
    for start, stop in ((first, rows), (0, first)):
        if stop > start:
            place = (start - first) % rows
            out_ref[(slice(place, place + stop - start), *where)] = value[start:stop]


def coefficients(bounds_ref, bands_ref, out_ref):
    tiles = bands_ref.shape[1]
    width = out_ref.shape[2]
    first = lax.axis_index("geo") * width
    column = first + lax.broadcasted_iota(jnp.int32, (tiles, width), 1)
    tile = jnp.zeros((tiles, width), jnp.int32)
    for j in range(1, tiles):
        tile = tile + (column >= bounds_ref[j]).astype(jnp.int32)
    own = (tile == lax.broadcasted_iota(jnp.int32, (tiles, width), 0)).astype(jnp.float32)
    own = own.astype(jnp.bfloat16)
    for k in range(out_ref.shape[0]):
        rest = bands_ref[k]
        value = 0.0
        for part in range(3):
            piece = rest.astype(jnp.bfloat16)
            rest = rest - piece.astype(jnp.float32)
            value = value + lax.dot_general(
                piece, own, (((0,), (0,)), ((), ())), preferred_element_type=jnp.float32
            )
        out_ref[k] = value


def diffuse_kernel(
    first,
    control_hbm,
    table_hbm,
    index_hbm,
    bounds_hbm,
    bands_hbm,
    out_ref,
    coef_ref,
    control_ref,
    table_ref,
    index_ref,
    bounds_ref,
    bands_ref,
    rows_ref,
    sems,
):
    copies = [
        pltpu.make_async_copy(source, target, sems.at[i])
        for i, (source, target) in enumerate(
            (
                (bounds_hbm, bounds_ref),
                (bands_hbm, bands_ref),
                (table_hbm, table_ref),
                (index_hbm, index_ref),
                (control_hbm, control_ref),
            )
        )
    ]
    for copy in copies:
        copy.start()
    levels, height, width = control_ref.shape[1:]
    groups = out_ref.shape[0]
    phases = height // groups
    tiles = width // LANES
    each = range(phases)

    def split(slot, load):
        for k in range(tiles):
            rows_ref[slot, k] = load(slice(k * LANES, (k + 1) * LANES))
        return [
            jnp.concatenate(
                [rows_ref[slot, k, pl.ds(r, groups, stride=phases), :] for k in range(tiles)],
                axis=1,
            )
            for r in each
        ]

    def kappa_of(lanes):
        index = index_ref[:, lanes]
        values = [table_ref[entry] for entry in range(table_ref.shape[0])]
        bit = 1
        while len(values) > 1:
            odd = (index & bit) != 0
            values = [jnp.where(odd, b, a) for a, b in zip(values[::2], values[1::2])]
            bit *= 2
        return values[0]

    def north_of(x):
        return pltpu.roll(x, width - 1, 1)

    def south_of(x):
        return pltpu.roll(x, 1, 1)

    def next_group(x):
        return pltpu.roll(x, groups - 1, 0)

    def previous_group(x):
        return pltpu.roll(x, 1, 0)

    copies[0].wait()
    copies[1].wait()
    coefficients(bounds_ref, bands_ref, coef_ref)
    copies[2].wait()
    copies[3].wait()
    kappa = split(levels, kappa_of)
    column = lax.broadcasted_iota(jnp.int32, (groups, width), 1)
    group = lax.broadcasted_iota(jnp.int32, (groups, width), 0)
    north = [jnp.where(column < width - 1, 0.5 * (k + north_of(k)), 0.0) for k in kappa]
    south = [south_of(w) for w in north]
    east = [0.5 * (kappa[r] + kappa[r + 1]) for r in range(phases - 1)]
    last = 0.5 * (kappa[-1] + next_group(kappa[0]))
    east.append(jnp.where(group < groups - 1, last, 0.0))
    west = [previous_group(east[-1])] + east[:-1]
    own = [1.0 - ((east[r] + west[r]) + (north[r] + south[r])) for r in each]

    def step(state):
        after = state[1:] + [next_group(state[0])]
        before = [previous_group(state[-1])] + state[:-1]
        return [
            (own[r] * state[r] + (east[r] * after[r] + west[r] * before[r]))
            + (north[r] * north_of(state[r]) + south[r] * south_of(state[r]))
            for r in each
        ]

    copies[4].wait()
    states = [split(v, lambda lanes: control_ref[0, v, :, lanes]) for v in range(levels)]
    for _ in range(ITERS):
        states = [step(state) for state in states]
    for level in range(levels):
        for r in each:
            lanes = slice(r * width, (r + 1) * width)
            store_turned(out_ref, states[level][r], first, level, lanes)


def diffuse(control, table, index, bounds, bands, groups, first):
    levels, height, width = control.shape[1:]
    share = height * width // groups
    arguments = [
        pltpu.with_memory_space_constraint(x, pltpu.HBM)
        for x in (control, table, index, bounds, bands)
    ]
    return pl.pallas_call(
        functools.partial(diffuse_kernel, first),
        out_shape=(
            jax.ShapeDtypeStruct((groups, levels, share), jnp.bfloat16),
            jax.ShapeDtypeStruct((bands.shape[0], bands.shape[2], share), jnp.float32),
        ),
        in_specs=[HBM] * 5,
        out_specs=(VMEM, VMEM),
        scratch_shapes=[
            pltpu.VMEM(control.shape, jnp.float32),
            pltpu.SMEM(table.shape, jnp.float32),
            pltpu.VMEM(index.shape, jnp.int32),
            pltpu.SMEM(bounds.shape, jnp.int32),
            pltpu.VMEM(bands.shape, jnp.float32),
            pltpu.VMEM((levels + 1, width // LANES, height, LANES), jnp.float32),
            pltpu.SemaphoreType.DMA((5,)),
        ],
        compiler_params=SMALL,
        name="diffuse",
    )(*arguments)


def product_kernel(geo_first, mem_first, state_ref, coef_ref, pert_ref, out_ref, pad_ref):
    shards, share, width = state_ref.shape
    levels = shards * share
    bands = coef_ref.shape[0]
    margin = 8
    for c in range(width // LANES):
        lanes = slice(c * LANES, (c + 1) * LANES)
        pad_ref[c, 0:margin] = jnp.zeros((margin, LANES), jnp.float32)
        pad_ref[c, margin + levels : 2 * margin + levels] = jnp.zeros((margin, LANES), jnp.float32)
        for place, g in enumerate(group_order(shards, geo_first)):
            rows = slice(margin + g * share, margin + (g + 1) * share)
            pad_ref[c, rows] = state_ref[place, :, lanes].astype(jnp.float32)
        value = pad_ref[c, margin : margin + levels]
        for k in range(bands):
            start = margin + k - bands // 2
            value = value + coef_ref[k, :, lanes] * pad_ref[c, start : start + levels]
        for v in range(2):
            product = pert_ref[v, 0, :, lanes].astype(jnp.float32) * value
            store_turned(out_ref, product, mem_first, v, lanes)


def products(state, coefs, perturbation, geo_first, mem_first):
    shards, share, width = state.shape
    levels = shards * share
    return pl.pallas_call(
        functools.partial(product_kernel, geo_first, mem_first),
        out_shape=jax.ShapeDtypeStruct((levels, 2, width), jnp.bfloat16),
        in_specs=[VMEM, VMEM, VMEM],
        out_specs=VMEM,
        scratch_shapes=[pltpu.VMEM((width // LANES, levels + 16, LANES), jnp.float32)],
        compiler_params=SMALL,
        name="products",
    )(state, coefs, perturbation)


def sum_kernel(terms_ref, out_ref):
    total = terms_ref[0].astype(jnp.float32)
    for m in range(1, terms_ref.shape[0]):
        total = total + terms_ref[m].astype(jnp.float32)
    for v in range(2):
        out_ref[v] = total[v : v + 1]


def member_sum(terms):
    return pl.pallas_call(
        sum_kernel,
        out_shape=jax.ShapeDtypeStruct((terms.shape[1], 1, terms.shape[2]), jnp.float32),
        in_specs=[VMEM],
        out_specs=VMEM,
        compiler_params=SMALL,
        name="member_sum",
    )(terms)


def exchange(x, axis, size, first):
    order = group_order(size, first)
    return lax.all_to_all(x, axis, 0, 0, axis_index_groups=[order], tiled=True)


def solution(mesh):
    groups, members = mesh.shape["geo"], mesh.shape["mem"]
    geo_first, mem_first = GEO_FIRST % groups, MEM_FIRST % members

    def body(control, kappa_table, kappa_index, tile_bounds, filter_bands, perturbation):
        bands = jnp.transpose(filter_bands, (1, 0, 2))
        sent, coefs = diffuse(
            control, kappa_table, kappa_index, tile_bounds, bands, groups, geo_first
        )
        state = exchange(sent, "geo", groups, geo_first)
        terms = products(state, coefs, perturbation, geo_first, mem_first)
        return member_sum(exchange(terms, "mem", members, mem_first))

    in_specs = (P("mem", "geo", None, None), P(), P(), P(), P(), P(None, "mem", None, "geo"))
    out_specs = P(None, "mem", "geo")
    return jax.shard_map(body, mesh=mesh, in_specs=in_specs, out_specs=out_specs, check_vma=False)
```

```python
import functools

import jax
import jax.numpy as jnp
from jax import lax
from jax.experimental import pallas as pl
from jax.experimental.pallas import tpu as pltpu
from jax.sharding import PartitionSpec as P

ITERS = 10
LANES = 128
GEO_FIRST = 9
MEM_FIRST = 26
HBM = pl.BlockSpec(memory_space=pltpu.HBM)
VMEM = pl.BlockSpec(memory_space=pltpu.VMEM)
SMALL = pltpu.CompilerParams(vmem_limit_bytes=4 << 20)


def group_order(size, first):
    return [(first - place) % size for place in range(size)]


def store_ordered(out_ref, value, order, *where):
    value = value.astype(out_ref.dtype)
    for place, row in enumerate(order):
        out_ref[(place, *where)] = value[row]


def coefficients(bounds_ref, bands_ref, out_ref):
    tiles = bands_ref.shape[1]
    width = out_ref.shape[2]
    first = lax.axis_index("geo") * width
    column = first + lax.broadcasted_iota(jnp.int32, (tiles, width), 1)
    tile = jnp.zeros((tiles, width), jnp.int32)
    for j in range(1, tiles):
        tile = tile + (column >= bounds_ref[j]).astype(jnp.int32)
    own = (tile == lax.broadcasted_iota(jnp.int32, (tiles, width), 0)).astype(jnp.float32)
    own = own.astype(jnp.bfloat16)
    for k in range(out_ref.shape[0]):
        rest = bands_ref[k]
        value = 0.0
        for part in range(3):
            piece = rest.astype(jnp.bfloat16)
            rest = rest - piece.astype(jnp.float32)
            value = value + lax.dot_general(
                piece, own, (((0,), (0,)), ((), ())), preferred_element_type=jnp.float32
            )
        out_ref[k] = value


def diffuse_kernel(
    order,
    control_hbm,
    table_hbm,
    index_hbm,
    bounds_hbm,
    bands_hbm,
    out_ref,
    coef_ref,
    control_ref,
    table_ref,
    index_ref,
    bounds_ref,
    bands_ref,
    rows_ref,
    sems,
):
    copies = [
        pltpu.make_async_copy(source, target, sems.at[i])
        for i, (source, target) in enumerate(
            (
                (bounds_hbm, bounds_ref),
                (bands_hbm, bands_ref),
                (table_hbm, table_ref),
                (index_hbm, index_ref),
                (control_hbm, control_ref),
            )
        )
    ]
    for copy in copies:
        copy.start()
    levels, height, width = control_ref.shape[1:]
    groups = out_ref.shape[0]
    phases = height // groups
    tiles = width // LANES
    each = range(phases)

    def split(slot, load):
        for k in range(tiles):
            rows_ref[slot, k] = load(slice(k * LANES, (k + 1) * LANES))
        return [
            jnp.concatenate(
                [rows_ref[slot, k, pl.ds(r, groups, stride=phases), :] for k in range(tiles)],
                axis=1,
            )
            for r in each
        ]

    def kappa_of(lanes):
        index = index_ref[:, lanes]
        values = [table_ref[entry] for entry in range(table_ref.shape[0])]
        bit = 1
        while len(values) > 1:
            odd = (index & bit) != 0
            values = [jnp.where(odd, b, a) for a, b in zip(values[::2], values[1::2])]
            bit *= 2
        return values[0]

    def north_of(x):
        return pltpu.roll(x, width - 1, 1)

    def south_of(x):
        return pltpu.roll(x, 1, 1)

    def next_group(x):
        return pltpu.roll(x, groups - 1, 0)

    def previous_group(x):
        return pltpu.roll(x, 1, 0)

    copies[2].wait()
    copies[3].wait()
    kappa = split(levels, kappa_of)
    column = lax.broadcasted_iota(jnp.int32, (groups, width), 1)
    group = lax.broadcasted_iota(jnp.int32, (groups, width), 0)
    north = [jnp.where(column < width - 1, 0.5 * (k + north_of(k)), 0.0) for k in kappa]
    south = [south_of(w) for w in north]
    east = [0.5 * (kappa[r] + kappa[r + 1]) for r in range(phases - 1)]
    last = 0.5 * (kappa[-1] + next_group(kappa[0]))
    east.append(jnp.where(group < groups - 1, last, 0.0))
    west = [previous_group(east[-1])] + east[:-1]
    own = [1.0 - ((east[r] + west[r]) + (north[r] + south[r])) for r in each]

    def step(state):
        after = state[1:] + [next_group(state[0])]
        before = [previous_group(state[-1])] + state[:-1]
        return [
            (own[r] * state[r] + (east[r] * after[r] + west[r] * before[r]))
            + (north[r] * north_of(state[r]) + south[r] * south_of(state[r]))
            for r in each
        ]

    copies[4].wait()
    copies[0].wait()
    copies[1].wait()
    coefficients(bounds_ref, bands_ref, coef_ref)
    states = [split(v, lambda lanes: control_ref[0, v, :, lanes]) for v in range(levels)]
    for _ in range(ITERS):
        states = [step(state) for state in states]
    for level in range(levels):
        for r in each:
            lanes = slice(r * width, (r + 1) * width)
            store_ordered(out_ref, states[level][r], order, level, lanes)


def diffuse(control, table, index, bounds, bands, order):
    levels, height, width = control.shape[1:]
    groups = len(order)
    share = height * width // groups
    arguments = [
        pltpu.with_memory_space_constraint(x, pltpu.HBM)
        for x in (control, table, index, bounds, bands)
    ]
    return pl.pallas_call(
        functools.partial(diffuse_kernel, order),
        out_shape=(
            jax.ShapeDtypeStruct((groups, levels, share), jnp.bfloat16),
            jax.ShapeDtypeStruct((bands.shape[0], bands.shape[2], share), jnp.float32),
        ),
        in_specs=[HBM] * 5,
        out_specs=(VMEM, VMEM),
        scratch_shapes=[
            pltpu.VMEM(control.shape, jnp.float32),
            pltpu.SMEM(table.shape, jnp.float32),
            pltpu.VMEM(index.shape, jnp.int32),
            pltpu.SMEM(bounds.shape, jnp.int32),
            pltpu.VMEM(bands.shape, jnp.float32),
            pltpu.VMEM((levels + 1, width // LANES, height, LANES), jnp.float32),
            pltpu.SemaphoreType.DMA((5,)),
        ],
        compiler_params=SMALL,
        name="diffuse",
    )(*arguments)


def product_kernel(geo_order, mem_order, state_ref, coef_ref, pert_ref, out_ref, pad_ref):
    shards, share, width = state_ref.shape
    levels = shards * share
    bands = coef_ref.shape[0]
    margin = 8
    for c in range(width // LANES):
        lanes = slice(c * LANES, (c + 1) * LANES)
        pad_ref[c, 0:margin] = jnp.zeros((margin, LANES), jnp.float32)
        pad_ref[c, margin + levels : 2 * margin + levels] = jnp.zeros((margin, LANES), jnp.float32)
        for place, g in enumerate(geo_order):
            rows = slice(margin + g * share, margin + (g + 1) * share)
            pad_ref[c, rows] = state_ref[place, :, lanes].astype(jnp.float32)
        value = pad_ref[c, margin : margin + levels]
        for k in range(bands):
            start = margin + k - bands // 2
            value = value + coef_ref[k, :, lanes] * pad_ref[c, start : start + levels]
        for v in range(2):
            product = pert_ref[v, 0, :, lanes].astype(jnp.float32) * value
            store_ordered(out_ref, product, mem_order, v, lanes)


def products(state, coefs, perturbation, geo_order, mem_order):
    shards, share, width = state.shape
    levels = shards * share
    return pl.pallas_call(
        functools.partial(product_kernel, geo_order, mem_order),
        out_shape=jax.ShapeDtypeStruct((levels, 2, width), jnp.bfloat16),
        in_specs=[VMEM, VMEM, VMEM],
        out_specs=VMEM,
        scratch_shapes=[pltpu.VMEM((width // LANES, levels + 16, LANES), jnp.float32)],
        compiler_params=SMALL,
        name="products",
    )(state, coefs, perturbation)


def sum_kernel(terms_ref, out_ref):
    total = terms_ref[0].astype(jnp.float32)
    for m in range(1, terms_ref.shape[0]):
        total = total + terms_ref[m].astype(jnp.float32)
    for v in range(2):
        out_ref[v] = total[v : v + 1]


def member_sum(terms):
    return pl.pallas_call(
        sum_kernel,
        out_shape=jax.ShapeDtypeStruct((terms.shape[1], 1, terms.shape[2]), jnp.float32),
        in_specs=[VMEM],
        out_specs=VMEM,
        compiler_params=SMALL,
        name="member_sum",
    )(terms)


def exchange(x, axis, order):
    return lax.all_to_all(x, axis, 0, 0, axis_index_groups=[order], tiled=True)


def solution(mesh):
    geo_order = group_order(mesh.shape["geo"], GEO_FIRST % mesh.shape["geo"])
    mem_order = group_order(mesh.shape["mem"], MEM_FIRST % mesh.shape["mem"])

    def body(control, kappa_table, kappa_index, tile_bounds, filter_bands, perturbation):
        bands = jnp.transpose(filter_bands, (1, 0, 2))
        sent, coefs = diffuse(control, kappa_table, kappa_index, tile_bounds, bands, geo_order)
        state = exchange(sent, "geo", geo_order)
        terms = products(state, coefs, perturbation, geo_order, mem_order)
        return member_sum(exchange(terms, "mem", mem_order))

    in_specs = (P("mem", "geo", None, None), P(), P(), P(), P(), P(None, "mem", None, "geo"))
    out_specs = P(None, "mem", "geo")
    return jax.shard_map(body, mesh=mesh, in_specs=in_specs, out_specs=out_specs, check_vma=False)
```

```python
import functools

import jax
import jax.numpy as jnp
from jax import lax
from jax.experimental import pallas as pl
from jax.experimental.pallas import tpu as pltpu
from jax.sharding import PartitionSpec as P

ITERS = 10
LANES = 128
GEO_FIRST = 9
MEM_FIRST = 26
HBM = pl.BlockSpec(memory_space=pltpu.HBM)
VMEM = pl.BlockSpec(memory_space=pltpu.VMEM)
SMALL = pltpu.CompilerParams(vmem_limit_bytes=4 << 20)


def group_order(size, first):
    return [(first - place) % size for place in range(size)]


def store_ordered(out_ref, value, order, *where):
    value = value.astype(out_ref.dtype)
    for place, row in enumerate(order):
        out_ref[(place, *where)] = value[row]


def coefficients(bounds_ref, bands_ref, out_ref):
    tiles = bands_ref.shape[1]
    width = out_ref.shape[2]
    first = lax.axis_index("geo") * width
    column = first + lax.broadcasted_iota(jnp.int32, (tiles, width), 1)
    tile = jnp.zeros((tiles, width), jnp.int32)
    for j in range(1, tiles):
        tile = tile + (column >= bounds_ref[j]).astype(jnp.int32)
    own = (tile == lax.broadcasted_iota(jnp.int32, (tiles, width), 0)).astype(jnp.float32)
    own = own.astype(jnp.bfloat16)
    for k in range(out_ref.shape[0]):
        rest = bands_ref[k]
        value = 0.0
        for part in range(3):
            piece = rest.astype(jnp.bfloat16)
            rest = rest - piece.astype(jnp.float32)
            value = value + lax.dot_general(
                piece, own, (((0,), (0,)), ((), ())), preferred_element_type=jnp.float32
            )
        out_ref[k] = value


def diffuse_kernel(
    order,
    control_hbm,
    table_hbm,
    index_hbm,
    bounds_hbm,
    bands_hbm,
    out_ref,
    coef_ref,
    control_ref,
    table_ref,
    index_ref,
    bounds_ref,
    bands_ref,
    rows_ref,
    sems,
):
    copies = [
        pltpu.make_async_copy(source, target, sems.at[i])
        for i, (source, target) in enumerate(
            (
                (index_hbm, index_ref),
                (table_hbm, table_ref),
                (control_hbm, control_ref),
                (bounds_hbm, bounds_ref),
                (bands_hbm, bands_ref),
            )
        )
    ]
    for copy in copies:
        copy.start()
    levels, height, width = control_ref.shape[1:]
    groups = out_ref.shape[0]
    phases = height // groups
    tiles = width // LANES
    each = range(phases)

    def split(slot, load):
        for k in range(tiles):
            rows_ref[slot, k] = load(slice(k * LANES, (k + 1) * LANES))
        return [
            jnp.concatenate(
                [rows_ref[slot, k, pl.ds(r, groups, stride=phases), :] for k in range(tiles)],
                axis=1,
            )
            for r in each
        ]

    def kappa_of(lanes):
        index = index_ref[:, lanes]
        values = [table_ref[entry] for entry in range(table_ref.shape[0])]
        bit = 1
        while len(values) > 1:
            odd = (index & bit) != 0
            values = [jnp.where(odd, b, a) for a, b in zip(values[::2], values[1::2])]
            bit *= 2
        return values[0]

    def north_of(x):
        return pltpu.roll(x, width - 1, 1)

    def south_of(x):
        return pltpu.roll(x, 1, 1)

    def next_group(x):
        return pltpu.roll(x, groups - 1, 0)

    def previous_group(x):
        return pltpu.roll(x, 1, 0)

    copies[1].wait()
    copies[0].wait()
    kappa = split(levels, kappa_of)
    column = lax.broadcasted_iota(jnp.int32, (groups, width), 1)
    group = lax.broadcasted_iota(jnp.int32, (groups, width), 0)
    north = [jnp.where(column < width - 1, 0.5 * (k + north_of(k)), 0.0) for k in kappa]
    south = [south_of(w) for w in north]
    east = [0.5 * (kappa[r] + kappa[r + 1]) for r in range(phases - 1)]
    last = 0.5 * (kappa[-1] + next_group(kappa[0]))
    east.append(jnp.where(group < groups - 1, last, 0.0))
    west = [previous_group(east[-1])] + east[:-1]
    own = [1.0 - ((east[r] + west[r]) + (north[r] + south[r])) for r in each]

    def step(state):
        after = state[1:] + [next_group(state[0])]
        before = [previous_group(state[-1])] + state[:-1]
        return [
            (own[r] * state[r] + (east[r] * after[r] + west[r] * before[r]))
            + (north[r] * north_of(state[r]) + south[r] * south_of(state[r]))
            for r in each
        ]

    copies[2].wait()
    copies[3].wait()
    copies[4].wait()
    coefficients(bounds_ref, bands_ref, coef_ref)
    states = [split(v, lambda lanes: control_ref[0, v, :, lanes]) for v in range(levels)]
    for _ in range(ITERS):
        states = [step(state) for state in states]
    for level in range(levels):
        for r in each:
            lanes = slice(r * width, (r + 1) * width)
            store_ordered(out_ref, states[level][r], order, level, lanes)


def diffuse(control, table, index, bounds, bands, order):
    levels, height, width = control.shape[1:]
    groups = len(order)
    share = height * width // groups
    arguments = [
        pltpu.with_memory_space_constraint(x, pltpu.HBM)
        for x in (control, table, index, bounds, bands)
    ]
    return pl.pallas_call(
        functools.partial(diffuse_kernel, order),
        out_shape=(
            jax.ShapeDtypeStruct((groups, levels, share), jnp.bfloat16),
            jax.ShapeDtypeStruct((bands.shape[0], bands.shape[2], share), jnp.float32),
        ),
        in_specs=[HBM] * 5,
        out_specs=(VMEM, VMEM),
        scratch_shapes=[
            pltpu.VMEM(control.shape, jnp.float32),
            pltpu.SMEM(table.shape, jnp.float32),
            pltpu.VMEM(index.shape, jnp.int32),
            pltpu.SMEM(bounds.shape, jnp.int32),
            pltpu.VMEM(bands.shape, jnp.float32),
            pltpu.VMEM((levels + 1, width // LANES, height, LANES), jnp.float32),
            pltpu.SemaphoreType.DMA((5,)),
        ],
        compiler_params=SMALL,
        name="diffuse",
    )(*arguments)


def product_kernel(geo_order, mem_order, state_ref, coef_ref, pert_ref, out_ref, pad_ref, pair_ref):
    shards, share, width = state_ref.shape
    levels = shards * share
    bands = coef_ref.shape[0]
    margin = 8
    for c in range(width // LANES):
        lanes = slice(c * LANES, (c + 1) * LANES)
        pad_ref[c, 0:margin] = jnp.zeros((margin, LANES), jnp.float32)
        pad_ref[c, margin + levels : 2 * margin + levels] = jnp.zeros((margin, LANES), jnp.float32)
        for place, g in enumerate(geo_order):
            rows = slice(margin + g * share, margin + (g + 1) * share)
            pad_ref[c, rows] = state_ref[place, :, lanes].astype(jnp.float32)
        value = pad_ref[c, margin : margin + levels]
        for k in range(bands):
            start = margin + k - bands // 2
            value = value + coef_ref[k, :, lanes] * pad_ref[c, start : start + levels]
        for v in range(2):
            product = pert_ref[v, 0, :, lanes].astype(jnp.float32) * value
            pair_ref[c, pl.ds(v, levels, stride=2), :] = product
        for place, level in enumerate(mem_order):
            pair = pair_ref[c, 2 * level : 2 * level + 2]
            out_ref[place, :, lanes] = pair.astype(jnp.bfloat16)


def products(state, coefs, perturbation, geo_order, mem_order):
    shards, share, width = state.shape
    levels = shards * share
    return pl.pallas_call(
        functools.partial(product_kernel, geo_order, mem_order),
        out_shape=jax.ShapeDtypeStruct((levels, 2, width), jnp.bfloat16),
        in_specs=[VMEM, VMEM, VMEM],
        out_specs=VMEM,
        scratch_shapes=[
            pltpu.VMEM((width // LANES, levels + 16, LANES), jnp.float32),
            pltpu.VMEM((width // LANES, 2 * levels, LANES), jnp.float32),
        ],
        compiler_params=SMALL,
        name="products",
    )(state, coefs, perturbation)


def sum_kernel(terms_ref, out_ref):
    total = terms_ref[0].astype(jnp.float32)
    for m in range(1, terms_ref.shape[0]):
        total = total + terms_ref[m].astype(jnp.float32)
    for v in range(2):
        out_ref[v] = total[v : v + 1]


def member_sum(terms):
    return pl.pallas_call(
        sum_kernel,
        out_shape=jax.ShapeDtypeStruct((terms.shape[1], 1, terms.shape[2]), jnp.float32),
        in_specs=[VMEM],
        out_specs=VMEM,
        compiler_params=SMALL,
        name="member_sum",
    )(terms)


def exchange(x, axis, order):
    return lax.all_to_all(x, axis, 0, 0, axis_index_groups=[order], tiled=True)


def solution(mesh):
    geo_order = group_order(mesh.shape["geo"], GEO_FIRST % mesh.shape["geo"])
    mem_order = group_order(mesh.shape["mem"], MEM_FIRST % mesh.shape["mem"])

    def body(control, kappa_table, kappa_index, tile_bounds, filter_bands, perturbation):
        bands = jnp.transpose(filter_bands, (1, 0, 2))
        sent, coefs = diffuse(control, kappa_table, kappa_index, tile_bounds, bands, geo_order)
        state = exchange(sent, "geo", geo_order)
        terms = products(state, coefs, perturbation, geo_order, mem_order)
        return member_sum(exchange(terms, "mem", mem_order))

    in_specs = (P("mem", "geo", None, None), P(), P(), P(), P(), P(None, "mem", None, "geo"))
    out_specs = P(None, "mem", "geo")
    return jax.shard_map(body, mesh=mesh, in_specs=in_specs, out_specs=out_specs, check_vma=False)
```

```python
import functools

import jax
import jax.numpy as jnp
from jax import lax
from jax.experimental import pallas as pl
from jax.experimental.pallas import tpu as pltpu
from jax.sharding import PartitionSpec as P

ITERS = 10
LANES = 128
SUBLANES = 8
GEO_FIRST = 9
MEM_FIRST = 26
HBM = pl.BlockSpec(memory_space=pltpu.HBM)
VMEM = pl.BlockSpec(memory_space=pltpu.VMEM)
SMALL = pltpu.CompilerParams(vmem_limit_bytes=4 << 20)


def group_order(size, first):
    return [(first - place) % size for place in range(size)]


def coefficients(bounds_ref, bands_ref, out_ref):
    tiles = bands_ref.shape[1]
    width = out_ref.shape[2]
    first = lax.axis_index("geo") * width
    column = first + lax.broadcasted_iota(jnp.int32, (tiles, width), 1)
    tile = jnp.zeros((tiles, width), jnp.int32)
    for j in range(1, tiles):
        tile = tile + (column >= bounds_ref[j]).astype(jnp.int32)
    own = (tile == lax.broadcasted_iota(jnp.int32, (tiles, width), 0)).astype(jnp.float32)
    own = own.astype(jnp.bfloat16)
    for k in range(out_ref.shape[0]):
        rest = bands_ref[k]
        value = 0.0
        for part in range(3):
            piece = rest.astype(jnp.bfloat16)
            rest = rest - piece.astype(jnp.float32)
            value = value + lax.dot_general(
                piece, own, (((0,), (0,)), ((), ())), preferred_element_type=jnp.float32
            )
        out_ref[k] = value


def diffuse_kernel(
    order,
    control_hbm,
    table_hbm,
    index_hbm,
    bounds_hbm,
    bands_hbm,
    out_ref,
    coef_ref,
    control_ref,
    table_ref,
    index_ref,
    bounds_ref,
    bands_ref,
    rows_ref,
    pair_ref,
    sems,
):
    copies = [
        pltpu.make_async_copy(source, target, sems.at[i])
        for i, (source, target) in enumerate(
            (
                (index_hbm, index_ref),
                (table_hbm, table_ref),
                (control_hbm, control_ref),
                (bounds_hbm, bounds_ref),
                (bands_hbm, bands_ref),
            )
        )
    ]
    for copy in copies:
        copy.start()
    levels, height, width = control_ref.shape[1:]
    groups = SUBLANES
    phases = height // groups
    band = height // out_ref.shape[0]
    tiles = width // LANES
    each = range(phases)

    def split(slot, load):
        for k in range(tiles):
            rows_ref[slot, k] = load(slice(k * LANES, (k + 1) * LANES))
        return [
            jnp.concatenate(
                [rows_ref[slot, k, pl.ds(r, groups, stride=phases), :] for k in range(tiles)],
                axis=1,
            )
            for r in each
        ]

    def kappa_of(lanes):
        index = index_ref[:, lanes]
        values = [table_ref[entry] for entry in range(table_ref.shape[0])]
        bit = 1
        while len(values) > 1:
            odd = (index & bit) != 0
            values = [jnp.where(odd, b, a) for a, b in zip(values[::2], values[1::2])]
            bit *= 2
        return values[0]

    def north_of(x):
        return pltpu.roll(x, width - 1, 1)

    def south_of(x):
        return pltpu.roll(x, 1, 1)

    def next_group(x):
        return pltpu.roll(x, groups - 1, 0)

    def previous_group(x):
        return pltpu.roll(x, 1, 0)

    copies[1].wait()
    copies[0].wait()
    kappa = split(levels, kappa_of)
    column = lax.broadcasted_iota(jnp.int32, (groups, width), 1)
    group = lax.broadcasted_iota(jnp.int32, (groups, width), 0)
    north = [jnp.where(column < width - 1, 0.5 * (k + north_of(k)), 0.0) for k in kappa]
    south = [south_of(w) for w in north]
    east = [0.5 * (kappa[r] + kappa[r + 1]) for r in range(phases - 1)]
    last = 0.5 * (kappa[-1] + next_group(kappa[0]))
    east.append(jnp.where(group < groups - 1, last, 0.0))
    west = [previous_group(east[-1])] + east[:-1]
    own = [1.0 - ((east[r] + west[r]) + (north[r] + south[r])) for r in each]

    def step(state):
        after = state[1:] + [next_group(state[0])]
        before = [previous_group(state[-1])] + state[:-1]
        return [
            (own[r] * state[r] + (east[r] * after[r] + west[r] * before[r]))
            + (north[r] * north_of(state[r]) + south[r] * south_of(state[r]))
            for r in each
        ]

    copies[2].wait()
    copies[3].wait()
    copies[4].wait()
    coefficients(bounds_ref, bands_ref, coef_ref)
    states = [split(v, lambda lanes: control_ref[0, v, :, lanes]) for v in range(levels)]
    for _ in range(ITERS):
        states = [step(state) for state in states]
    share = phases // band
    for r in each:
        for k in range(tiles):
            for v in range(levels):
                piece = states[v][r][:, k * LANES : (k + 1) * LANES]
                pair_ref[r, k, pl.ds(v, groups, stride=levels), :] = piece
    for r in each:
        for k in range(tiles):
            start = r % band * width + k * LANES
            lanes = slice(start, start + LANES)
            for g in range(groups):
                pair = pair_ref[r, k, g * levels : (g + 1) * levels]
                place = order.index(g * share + r // band)
                out_ref[place, :, lanes] = pair.astype(jnp.bfloat16)


def diffuse(control, table, index, bounds, bands, order):
    levels, height, width = control.shape[1:]
    groups = len(order)
    share = height * width // groups
    arguments = [
        pltpu.with_memory_space_constraint(x, pltpu.HBM)
        for x in (control, table, index, bounds, bands)
    ]
    return pl.pallas_call(
        functools.partial(diffuse_kernel, order),
        out_shape=(
            jax.ShapeDtypeStruct((groups, levels, share), jnp.bfloat16),
            jax.ShapeDtypeStruct((bands.shape[0], bands.shape[2], share), jnp.float32),
        ),
        in_specs=[HBM] * 5,
        out_specs=(VMEM, VMEM),
        scratch_shapes=[
            pltpu.VMEM(control.shape, jnp.float32),
            pltpu.SMEM(table.shape, jnp.float32),
            pltpu.VMEM(index.shape, jnp.int32),
            pltpu.SMEM(bounds.shape, jnp.int32),
            pltpu.VMEM(bands.shape, jnp.float32),
            pltpu.VMEM((levels + 1, width // LANES, height, LANES), jnp.float32),
            pltpu.VMEM((height // SUBLANES, width // LANES, SUBLANES * levels, LANES), jnp.float32),
            pltpu.SemaphoreType.DMA((5,)),
        ],
        compiler_params=SMALL,
        name="diffuse",
    )(*arguments)


def product_kernel(geo_order, mem_order, state_ref, coef_ref, pert_ref, out_ref, pad_ref, pair_ref):
    shards, share, width = state_ref.shape
    levels = shards * share
    bands = coef_ref.shape[0]
    margin = 8
    for c in range(width // LANES):
        lanes = slice(c * LANES, (c + 1) * LANES)
        pad_ref[c, 0:margin] = jnp.zeros((margin, LANES), jnp.float32)
        pad_ref[c, margin + levels : 2 * margin + levels] = jnp.zeros((margin, LANES), jnp.float32)
        for place, g in enumerate(geo_order):
            rows = slice(margin + g * share, margin + (g + 1) * share)
            pad_ref[c, rows] = state_ref[place, :, lanes].astype(jnp.float32)
        value = pad_ref[c, margin : margin + levels]
        for k in range(bands):
            start = margin + k - bands // 2
            value = value + coef_ref[k, :, lanes] * pad_ref[c, start : start + levels]
        for v in range(2):
            product = pert_ref[v, 0, :, lanes].astype(jnp.float32) * value
            pair_ref[c, pl.ds(v, levels, stride=2), :] = product
        for place, level in enumerate(mem_order):
            pair = pair_ref[c, 2 * level : 2 * level + 2]
            out_ref[place, :, lanes] = pair.astype(jnp.bfloat16)


def products(state, coefs, perturbation, geo_order, mem_order):
    shards, share, width = state.shape
    levels = shards * share
    return pl.pallas_call(
        functools.partial(product_kernel, geo_order, mem_order),
        out_shape=jax.ShapeDtypeStruct((levels, 2, width), jnp.bfloat16),
        in_specs=[VMEM, VMEM, VMEM],
        out_specs=VMEM,
        scratch_shapes=[
            pltpu.VMEM((width // LANES, levels + 16, LANES), jnp.float32),
            pltpu.VMEM((width // LANES, 2 * levels, LANES), jnp.float32),
        ],
        compiler_params=SMALL,
        name="products",
    )(state, coefs, perturbation)


def sum_kernel(terms_ref, out_ref):
    total = terms_ref[0].astype(jnp.float32)
    for m in range(1, terms_ref.shape[0]):
        total = total + terms_ref[m].astype(jnp.float32)
    for v in range(2):
        out_ref[v] = total[v : v + 1]


def member_sum(terms):
    return pl.pallas_call(
        sum_kernel,
        out_shape=jax.ShapeDtypeStruct((terms.shape[1], 1, terms.shape[2]), jnp.float32),
        in_specs=[VMEM],
        out_specs=VMEM,
        compiler_params=SMALL,
        name="member_sum",
    )(terms)


def exchange(x, axis, order):
    return lax.all_to_all(x, axis, 0, 0, axis_index_groups=[order], tiled=True)


def solution(mesh):
    geo_order = group_order(mesh.shape["geo"], GEO_FIRST % mesh.shape["geo"])
    mem_order = group_order(mesh.shape["mem"], MEM_FIRST % mesh.shape["mem"])

    def body(control, kappa_table, kappa_index, tile_bounds, filter_bands, perturbation):
        bands = jnp.transpose(filter_bands, (1, 0, 2))
        sent, coefs = diffuse(control, kappa_table, kappa_index, tile_bounds, bands, geo_order)
        state = exchange(sent, "geo", geo_order)
        terms = products(state, coefs, perturbation, geo_order, mem_order)
        return member_sum(exchange(terms, "mem", mem_order))

    in_specs = (P("mem", "geo", None, None), P(), P(), P(), P(), P(None, "mem", None, "geo"))
    out_specs = P(None, "mem", "geo")
    return jax.shard_map(body, mesh=mesh, in_specs=in_specs, out_specs=out_specs, check_vma=False)
```

```python
import functools

import jax
import jax.numpy as jnp
from jax import lax
from jax.experimental import pallas as pl
from jax.experimental.pallas import tpu as pltpu
from jax.sharding import PartitionSpec as P

ITERS = 10
LANES = 128
SUBLANES = 8
GEO_FIRST = 9
MEM_FIRST = 26
HBM = pl.BlockSpec(memory_space=pltpu.HBM)
VMEM = pl.BlockSpec(memory_space=pltpu.VMEM)
SMALL = pltpu.CompilerParams(vmem_limit_bytes=4 << 20)


def group_order(size, first):
    return [(first - place) % size for place in range(size)]


def coefficients(bounds_ref, bands_ref, out_ref):
    tiles = bands_ref.shape[1]
    width = out_ref.shape[2]
    first = lax.axis_index("geo") * width
    column = first + lax.broadcasted_iota(jnp.int32, (tiles, width), 1)
    tile = jnp.zeros((tiles, width), jnp.int32)
    for j in range(1, tiles):
        tile = tile + (column >= bounds_ref[j]).astype(jnp.int32)
    own = (tile == lax.broadcasted_iota(jnp.int32, (tiles, width), 0)).astype(jnp.float32)
    own = own.astype(jnp.bfloat16)
    for k in range(out_ref.shape[0]):
        rest = bands_ref[k]
        value = 0.0
        for part in range(3):
            piece = rest.astype(jnp.bfloat16)
            rest = rest - piece.astype(jnp.float32)
            value = value + lax.dot_general(
                piece, own, (((0,), (0,)), ((), ())), preferred_element_type=jnp.float32
            )
        out_ref[k] = value


def diffuse_kernel(
    order,
    control_hbm,
    table_hbm,
    index_hbm,
    bounds_hbm,
    bands_hbm,
    pert_hbm,
    out_ref,
    coef_ref,
    pert_ref,
    control_ref,
    table_ref,
    index_ref,
    bounds_ref,
    bands_ref,
    rows_ref,
    pair_ref,
    sems,
):
    copies = [
        pltpu.make_async_copy(source, target, sems.at[i])
        for i, (source, target) in enumerate(
            (
                (index_hbm, index_ref),
                (table_hbm, table_ref),
                (control_hbm, control_ref),
                (bounds_hbm, bounds_ref),
                (bands_hbm, bands_ref),
            )
        )
    ]
    for copy in copies:
        copy.start()
    levels, height, width = control_ref.shape[1:]
    groups = SUBLANES
    phases = height // groups
    band = height // out_ref.shape[0]
    tiles = width // LANES
    each = range(phases)

    def split(slot, load):
        for k in range(tiles):
            rows_ref[slot, k] = load(slice(k * LANES, (k + 1) * LANES))
        return [
            jnp.concatenate(
                [rows_ref[slot, k, pl.ds(r, groups, stride=phases), :] for k in range(tiles)],
                axis=1,
            )
            for r in each
        ]

    def kappa_of(lanes):
        index = index_ref[:, lanes]
        values = [table_ref[entry] for entry in range(table_ref.shape[0])]
        bit = 1
        while len(values) > 1:
            odd = (index & bit) != 0
            values = [jnp.where(odd, b, a) for a, b in zip(values[::2], values[1::2])]
            bit *= 2
        return values[0]

    def north_of(x):
        return pltpu.roll(x, width - 1, 1)

    def south_of(x):
        return pltpu.roll(x, 1, 1)

    def next_group(x):
        return pltpu.roll(x, groups - 1, 0)

    def previous_group(x):
        return pltpu.roll(x, 1, 0)

    copies[1].wait()
    copies[0].wait()
    kappa = split(levels, kappa_of)
    column = lax.broadcasted_iota(jnp.int32, (groups, width), 1)
    group = lax.broadcasted_iota(jnp.int32, (groups, width), 0)
    north = [jnp.where(column < width - 1, 0.5 * (k + north_of(k)), 0.0) for k in kappa]
    south = [south_of(w) for w in north]
    east = [0.5 * (kappa[r] + kappa[r + 1]) for r in range(phases - 1)]
    last = 0.5 * (kappa[-1] + next_group(kappa[0]))
    east.append(jnp.where(group < groups - 1, last, 0.0))
    west = [previous_group(east[-1])] + east[:-1]
    own = [1.0 - ((east[r] + west[r]) + (north[r] + south[r])) for r in each]

    def step(state):
        after = state[1:] + [next_group(state[0])]
        before = [previous_group(state[-1])] + state[:-1]
        return [
            (own[r] * state[r] + (east[r] * after[r] + west[r] * before[r]))
            + (north[r] * north_of(state[r]) + south[r] * south_of(state[r]))
            for r in each
        ]

    copies[2].wait()
    pert_copy = pltpu.make_async_copy(pert_hbm, pert_ref, sems.at[5])
    pert_copy.start()
    copies[3].wait()
    copies[4].wait()
    coefficients(bounds_ref, bands_ref, coef_ref)
    states = [split(v, lambda lanes: control_ref[0, v, :, lanes]) for v in range(levels)]
    for _ in range(ITERS):
        states = [step(state) for state in states]
    share = phases // band
    for r in each:
        for k in range(tiles):
            for v in range(levels):
                piece = states[v][r][:, k * LANES : (k + 1) * LANES]
                pair_ref[r, k, pl.ds(v, groups, stride=levels), :] = piece
    for r in each:
        for k in range(tiles):
            start = r % band * width + k * LANES
            lanes = slice(start, start + LANES)
            for g in range(groups):
                pair = pair_ref[r, k, g * levels : (g + 1) * levels]
                place = order.index(g * share + r // band)
                out_ref[place, :, lanes] = pair.astype(jnp.bfloat16)
    pert_copy.wait()


def diffuse(control, table, index, bounds, bands, perturbation, order):
    levels, height, width = control.shape[1:]
    groups = len(order)
    share = height * width // groups
    arguments = [
        pltpu.with_memory_space_constraint(x, pltpu.HBM)
        for x in (control, table, index, bounds, bands, perturbation)
    ]
    return pl.pallas_call(
        functools.partial(diffuse_kernel, order),
        out_shape=(
            jax.ShapeDtypeStruct((groups, levels, share), jnp.bfloat16),
            jax.ShapeDtypeStruct((bands.shape[0], bands.shape[2], share), jnp.float32),
            jax.ShapeDtypeStruct(perturbation.shape, perturbation.dtype),
        ),
        in_specs=[HBM] * 6,
        out_specs=(VMEM, VMEM, VMEM),
        scratch_shapes=[
            pltpu.VMEM(control.shape, jnp.float32),
            pltpu.SMEM(table.shape, jnp.float32),
            pltpu.VMEM(index.shape, jnp.int32),
            pltpu.SMEM(bounds.shape, jnp.int32),
            pltpu.VMEM(bands.shape, jnp.float32),
            pltpu.VMEM((levels + 1, width // LANES, height, LANES), jnp.float32),
            pltpu.VMEM((height // SUBLANES, width // LANES, SUBLANES * levels, LANES), jnp.float32),
            pltpu.SemaphoreType.DMA((6,)),
        ],
        compiler_params=SMALL,
        name="diffuse",
    )(*arguments)


def product_kernel(geo_order, mem_order, state_ref, coef_ref, pert_ref, out_ref, pad_ref, pair_ref):
    shards, share, width = state_ref.shape
    levels = shards * share
    bands = coef_ref.shape[0]
    margin = 8
    for c in range(width // LANES):
        lanes = slice(c * LANES, (c + 1) * LANES)
        pad_ref[c, 0:margin] = jnp.zeros((margin, LANES), jnp.float32)
        pad_ref[c, margin + levels : 2 * margin + levels] = jnp.zeros((margin, LANES), jnp.float32)
        for place, g in enumerate(geo_order):
            rows = slice(margin + g * share, margin + (g + 1) * share)
            pad_ref[c, rows] = state_ref[place, :, lanes].astype(jnp.float32)
        value = pad_ref[c, margin : margin + levels]
        for k in range(bands):
            start = margin + k - bands // 2
            value = value + coef_ref[k, :, lanes] * pad_ref[c, start : start + levels]
        for v in range(2):
            product = pert_ref[v, 0, :, lanes].astype(jnp.float32) * value
            pair_ref[c, pl.ds(v, levels, stride=2), :] = product
        for place, level in enumerate(mem_order):
            pair = pair_ref[c, 2 * level : 2 * level + 2]
            out_ref[place, :, lanes] = pair.astype(jnp.bfloat16)


def products(state, coefs, perturbation, geo_order, mem_order):
    shards, share, width = state.shape
    levels = shards * share
    return pl.pallas_call(
        functools.partial(product_kernel, geo_order, mem_order),
        out_shape=jax.ShapeDtypeStruct((levels, 2, width), jnp.bfloat16),
        in_specs=[VMEM, VMEM, VMEM],
        out_specs=VMEM,
        scratch_shapes=[
            pltpu.VMEM((width // LANES, levels + 16, LANES), jnp.float32),
            pltpu.VMEM((width // LANES, 2 * levels, LANES), jnp.float32),
        ],
        compiler_params=SMALL,
        name="products",
    )(state, coefs, perturbation)


def sum_kernel(terms_ref, out_ref):
    total = terms_ref[0].astype(jnp.float32)
    for m in range(1, terms_ref.shape[0]):
        total = total + terms_ref[m].astype(jnp.float32)
    for v in range(2):
        out_ref[v] = total[v : v + 1]


def member_sum(terms):
    return pl.pallas_call(
        sum_kernel,
        out_shape=jax.ShapeDtypeStruct((terms.shape[1], 1, terms.shape[2]), jnp.float32),
        in_specs=[VMEM],
        out_specs=VMEM,
        compiler_params=SMALL,
        name="member_sum",
    )(terms)


def exchange(x, axis, order):
    return lax.all_to_all(x, axis, 0, 0, axis_index_groups=[order], tiled=True)


def solution(mesh):
    geo_order = group_order(mesh.shape["geo"], GEO_FIRST % mesh.shape["geo"])
    mem_order = group_order(mesh.shape["mem"], MEM_FIRST % mesh.shape["mem"])

    def body(control, kappa_table, kappa_index, tile_bounds, filter_bands, perturbation):
        bands = jnp.transpose(filter_bands, (1, 0, 2))
        sent, coefs, pert = diffuse(
            control, kappa_table, kappa_index, tile_bounds, bands, perturbation, geo_order
        )
        state = exchange(sent, "geo", geo_order)
        terms = products(state, coefs, pert, geo_order, mem_order)
        return member_sum(exchange(terms, "mem", mem_order))

    in_specs = (P("mem", "geo", None, None), P(), P(), P(), P(), P(None, "mem", None, "geo"))
    out_specs = P(None, "mem", "geo")
    return jax.shard_map(body, mesh=mesh, in_specs=in_specs, out_specs=out_specs, check_vma=False)
```

```python
import functools

import jax
import jax.numpy as jnp
from jax import lax
from jax.experimental import pallas as pl
from jax.experimental.pallas import tpu as pltpu
from jax.sharding import PartitionSpec as P

ITERS = 10
LANES = 128
SUBLANES = 8
GEO_FIRST = 9
MEM_FIRST = 26
HBM = pl.BlockSpec(memory_space=pltpu.HBM)
VMEM = pl.BlockSpec(memory_space=pltpu.VMEM)
SMALL = pltpu.CompilerParams(vmem_limit_bytes=4 << 20)


def group_order(size, first):
    return [(first - place) % size for place in range(size)]


def coefficients(bounds_ref, bands_ref, out_ref):
    tiles = bands_ref.shape[1]
    width = out_ref.shape[2]
    first = lax.axis_index("geo") * width
    column = first + lax.broadcasted_iota(jnp.int32, (tiles, width), 1)
    tile = jnp.zeros((tiles, width), jnp.int32)
    for j in range(1, tiles):
        tile = tile + (column >= bounds_ref[j]).astype(jnp.int32)
    own = (tile == lax.broadcasted_iota(jnp.int32, (tiles, width), 0)).astype(jnp.float32)
    own = own.astype(jnp.bfloat16)
    for k in range(out_ref.shape[0]):
        rest = bands_ref[k]
        value = 0.0
        for part in range(3):
            piece = rest.astype(jnp.bfloat16)
            rest = rest - piece.astype(jnp.float32)
            value = value + lax.dot_general(
                piece, own, (((0,), (0,)), ((), ())), preferred_element_type=jnp.float32
            )
        out_ref[k] = value


def diffuse_kernel(
    order,
    control_hbm,
    table_hbm,
    index_hbm,
    bounds_hbm,
    bands_hbm,
    pert_hbm,
    out_ref,
    coef_ref,
    pert_ref,
    control_ref,
    table_ref,
    index_ref,
    bounds_ref,
    bands_ref,
    rows_ref,
    pair_ref,
    sems,
):
    copies = [
        pltpu.make_async_copy(source, target, sems.at[i])
        for i, (source, target) in enumerate(
            (
                (index_hbm, index_ref),
                (table_hbm, table_ref),
                (control_hbm, control_ref),
                (bounds_hbm, bounds_ref),
                (bands_hbm, bands_ref),
            )
        )
    ]
    for copy in copies:
        copy.start()
    levels, height, width = control_ref.shape[1:]
    groups = SUBLANES
    phases = height // groups
    band = height // out_ref.shape[0]
    tiles = width // LANES
    each = range(phases)

    def split(slot, load):
        for k in range(tiles):
            rows_ref[slot, k] = load(slice(k * LANES, (k + 1) * LANES))
        return [
            jnp.concatenate(
                [rows_ref[slot, k, pl.ds(r, groups, stride=phases), :] for k in range(tiles)],
                axis=1,
            )
            for r in each
        ]

    def kappa_of(lanes):
        index = index_ref[:, lanes]
        values = [table_ref[entry] for entry in range(table_ref.shape[0])]
        bit = 1
        while len(values) > 1:
            odd = (index & bit) != 0
            values = [jnp.where(odd, b, a) for a, b in zip(values[::2], values[1::2])]
            bit *= 2
        return values[0]

    def north_of(x):
        return pltpu.roll(x, width - 1, 1)

    def south_of(x):
        return pltpu.roll(x, 1, 1)

    def next_group(x):
        return pltpu.roll(x, groups - 1, 0)

    def previous_group(x):
        return pltpu.roll(x, 1, 0)

    copies[1].wait()
    copies[0].wait()
    kappa = split(levels, kappa_of)
    column = lax.broadcasted_iota(jnp.int32, (groups, width), 1)
    group = lax.broadcasted_iota(jnp.int32, (groups, width), 0)
    north = [jnp.where(column < width - 1, 0.5 * (k + north_of(k)), 0.0) for k in kappa]
    south = [south_of(w) for w in north]
    east = [0.5 * (kappa[r] + kappa[r + 1]) for r in range(phases - 1)]
    last = 0.5 * (kappa[-1] + next_group(kappa[0]))
    east.append(jnp.where(group < groups - 1, last, 0.0))
    west = [previous_group(east[-1])] + east[:-1]
    own = [1.0 - ((east[r] + west[r]) + (north[r] + south[r])) for r in each]

    def step(state):
        after = state[1:] + [next_group(state[0])]
        before = [previous_group(state[-1])] + state[:-1]
        return [
            (own[r] * state[r] + (east[r] * after[r] + west[r] * before[r]))
            + (north[r] * north_of(state[r]) + south[r] * south_of(state[r]))
            for r in each
        ]

    copies[2].wait()
    pert_copy = pltpu.make_async_copy(pert_hbm, pert_ref, sems.at[5])
    pert_copy.start()
    copies[3].wait()
    copies[4].wait()
    coefficients(bounds_ref, bands_ref, coef_ref)
    states = [split(v, lambda lanes: control_ref[0, v, :, lanes]) for v in range(levels)]
    for _ in range(ITERS):
        states = [step(state) for state in states]
    share = phases // band
    for r in each:
        for k in range(tiles):
            for v in range(levels):
                piece = states[v][r][:, k * LANES : (k + 1) * LANES]
                pair_ref[r, k, pl.ds(v, groups, stride=levels), :] = piece
    for r in each:
        for k in range(tiles):
            start = r % band * width + k * LANES
            lanes = slice(start, start + LANES)
            for g in range(groups):
                pair = pair_ref[r, k, g * levels : (g + 1) * levels]
                place = order.index(g * share + r // band)
                out_ref[place, :, lanes] = pair.astype(jnp.bfloat16)
    pert_copy.wait()


def diffuse(control, table, index, bounds, bands, perturbation, order):
    levels, height, width = control.shape[1:]
    groups = len(order)
    share = height * width // groups
    arguments = [
        pltpu.with_memory_space_constraint(x, pltpu.HBM)
        for x in (control, table, index, bounds, bands, perturbation)
    ]
    return pl.pallas_call(
        functools.partial(diffuse_kernel, order),
        out_shape=(
            jax.ShapeDtypeStruct((groups, levels, share), jnp.bfloat16),
            jax.ShapeDtypeStruct((bands.shape[0], bands.shape[2], share), jnp.float32),
            jax.ShapeDtypeStruct(perturbation.shape, perturbation.dtype),
        ),
        in_specs=[HBM] * 6,
        out_specs=(VMEM, VMEM, VMEM),
        scratch_shapes=[
            pltpu.VMEM(control.shape, jnp.float32),
            pltpu.SMEM(table.shape, jnp.float32),
            pltpu.VMEM(index.shape, jnp.int32),
            pltpu.SMEM(bounds.shape, jnp.int32),
            pltpu.VMEM(bands.shape, jnp.float32),
            pltpu.VMEM((levels + 1, width // LANES, height, LANES), jnp.float32),
            pltpu.VMEM((height // SUBLANES, width // LANES, SUBLANES * levels, LANES), jnp.float32),
            pltpu.SemaphoreType.DMA((6,)),
        ],
        compiler_params=SMALL,
        name="diffuse",
    )(*arguments)


def product_kernel(geo_order, mem_order, state_ref, coef_ref, pert_ref, out_ref, pad_ref, pair_ref):
    shards, share, width = state_ref.shape
    levels = shards * share
    bands = coef_ref.shape[0]
    margin = 8
    for c in range(width // LANES):
        lanes = slice(c * LANES, (c + 1) * LANES)
        pad_ref[c, 0:margin] = jnp.zeros((margin, LANES), jnp.float32)
        pad_ref[c, margin + levels : 2 * margin + levels] = jnp.zeros((margin, LANES), jnp.float32)
        for place, g in enumerate(geo_order):
            rows = slice(margin + g * share, margin + (g + 1) * share)
            pad_ref[c, rows] = state_ref[place, :, lanes].astype(jnp.float32)
        value = pad_ref[c, margin : margin + levels]
        for k in range(bands):
            start = margin + k - bands // 2
            value = value + coef_ref[k, :, lanes] * pad_ref[c, start : start + levels]
        for v in range(2):
            product = pert_ref[v, 0, :, lanes].astype(jnp.float32) * value
            pair_ref[c, pl.ds(v, levels, stride=2), :] = product
        for place, level in enumerate(mem_order):
            pair = pair_ref[c, 2 * level : 2 * level + 2]
            out_ref[place, :, lanes] = pair.astype(jnp.bfloat16)


def products(state, coefs, perturbation, geo_order, mem_order):
    shards, share, width = state.shape
    levels = shards * share
    return pl.pallas_call(
        functools.partial(product_kernel, geo_order, mem_order),
        out_shape=jax.ShapeDtypeStruct((levels, 2, width), jnp.bfloat16),
        in_specs=[VMEM, VMEM, VMEM],
        out_specs=VMEM,
        scratch_shapes=[
            pltpu.VMEM((width // LANES, levels + 16, LANES), jnp.float32),
            pltpu.VMEM((width // LANES, 2 * levels, LANES), jnp.float32),
        ],
        compiler_params=SMALL,
        name="products",
    )(state, coefs, perturbation)


def sum_kernel(terms_ref, out_ref):
    members = terms_ref.shape[0]
    chains = [terms_ref[m].astype(jnp.float32) for m in range(4)]
    for m in range(4, members):
        chains[m % 4] = chains[m % 4] + terms_ref[m].astype(jnp.float32)
    total = (chains[0] + chains[1]) + (chains[2] + chains[3])
    for v in range(2):
        out_ref[v] = total[v : v + 1]


def member_sum(terms):
    return pl.pallas_call(
        sum_kernel,
        out_shape=jax.ShapeDtypeStruct((terms.shape[1], 1, terms.shape[2]), jnp.float32),
        in_specs=[VMEM],
        out_specs=VMEM,
        compiler_params=SMALL,
        name="member_sum",
    )(terms)


def exchange(x, axis, order):
    return lax.all_to_all(x, axis, 0, 0, axis_index_groups=[order], tiled=True)


def solution(mesh):
    geo_order = group_order(mesh.shape["geo"], GEO_FIRST % mesh.shape["geo"])
    mem_order = group_order(mesh.shape["mem"], MEM_FIRST % mesh.shape["mem"])

    def body(control, kappa_table, kappa_index, tile_bounds, filter_bands, perturbation):
        bands = jnp.transpose(filter_bands, (1, 0, 2))
        sent, coefs, pert = diffuse(
            control, kappa_table, kappa_index, tile_bounds, bands, perturbation, geo_order
        )
        state = exchange(sent, "geo", geo_order)
        terms = products(state, coefs, pert, geo_order, mem_order)
        return member_sum(exchange(terms, "mem", mem_order))

    in_specs = (P("mem", "geo", None, None), P(), P(), P(), P(), P(None, "mem", None, "geo"))
    out_specs = P(None, "mem", "geo")
    return jax.shard_map(body, mesh=mesh, in_specs=in_specs, out_specs=out_specs, check_vma=False)
```
